512 devices in a mesh: range: 16 (over y, core), date: 32 (over z, x).
Axes of the slice: x: 4, y: 8, z: 8, core: 2. Of those that a mesh axis runs over, the one named last changes fastest.
Arguments:
- slc: bfloat16 [2, 128, 128, 10240], P(None, 'date', None, 'range'), may hold values from -12 to 12
- row_offset: int32 [128], P('date'), may hold values from -16 to 15
- col_offset: int32 [128], P('date'), may hold values from -16 to 15
- valid: int32 [32, 512, 128], P('date', 'range'), may hold values 0 or 1
Outputs:
- coherence: bfloat16 [32, 512, 128, 128], P('date', 'range')
- pair_coherence: float32 [32, 512, 4, 2, 128], P('date', 'range')
The draws below stay inside these ranges and needn't reach their ends.
Inputs may be any that keep to these rules, and one draw needn't show every extreme that they name: `row_offset`: offsets in eighths of a cell. `col_offset`: offsets in eighths of a cell.
All inputs are finite; a program needn't handle non-finite values. No bound on the sum of `valid` on one device may be relied on, other than what follows from the above.
Results may differ from the reference program's by a relative error of at most 0.0048.
Values may be sent and summed in bfloat16 or wider, within the bound.
A program may use at most 128 MiB of HBM per device.

```python
import jax
import jax.numpy as jnp
from jax import lax

AZ = 128
PAIRS = 4
DATES = 128
COLS = 10240
MLAZ = 32
MLRG = 512


def draw_slc(key, part):
    key = jax.random.fold_in(key, 11)
    first, second = jax.random.split(key, 2)
    common = jax.random.truncated_normal(first, -4.0, 4.0, (2, 1, AZ, COLS), jnp.float32)
    noise = jax.random.truncated_normal(second, -4.0, 4.0, (2, DATES, AZ, COLS), jnp.float32)
    return (common + noise).astype(jnp.bfloat16)


def set_ends(result, key, smallest, high):
    spot = [jax.random.randint(jax.random.fold_in(key, axis), (), 0, length) for axis, length in enumerate(result.shape)]
    widest = result.shape.index(max(result.shape))
    neighbour = spot[:widest] + [(spot[widest] + 1) % result.shape[widest]] + spot[widest + 1:]
    return result.at[tuple(spot)].set(smallest).at[tuple(neighbour)].set(high)


def setup_inputs(seed: int = 0) -> dict:
    arg_keys = jax.random.split(jax.random.key(seed), 5)
    return {
        "slc": draw_slc(jax.random.fold_in(arg_keys[4], 71), 0),
        "row_offset": set_ends(jax.random.randint(arg_keys[1], (DATES,), -16, 16), jax.random.fold_in(arg_keys[1], 1), -16, 15).astype(jnp.int32),
        "col_offset": set_ends(jax.random.randint(arg_keys[2], (DATES,), -16, 16), jax.random.fold_in(arg_keys[2], 1), -16, 15).astype(jnp.int32),
        "valid": set_ends((jax.random.randint(arg_keys[3], (MLAZ, MLRG, DATES), 0, 8) < 7).astype(jnp.int32), jax.random.fold_in(arg_keys[3], 1), 0, 1),
    }


def lanczos(values):
    return jnp.where(jnp.abs(values) < 4.0, jnp.sinc(values) * jnp.sinc(values / 4.0), 0.0)

def tap_weights(offset):
    shift = offset.astype(jnp.float32) / 8.0
    taps = jnp.arange(-5, 6).astype(jnp.float32)
    return lanczos(shift[:, None] - taps[None, :]).astype(jnp.bfloat16)

def resample_one(packed):
    image, rweights, cweights = packed
    padded = jnp.pad(image, ((0, 0), (0, 0), (5, 5))).astype(jnp.float32)
    total = jnp.zeros(image.shape, jnp.float32)
    for tap in range(11):
        total = total + cweights[tap].astype(jnp.float32) * padded[:, :, tap:tap + COLS]
    across = total.astype(jnp.bfloat16)
    padded = jnp.pad(across, ((0, 0), (5, 5), (0, 0))).astype(jnp.float32)
    total = jnp.zeros(image.shape, jnp.float32)
    for tap in range(11):
        total = total + rweights[tap].astype(jnp.float32) * padded[:, tap:tap + AZ, :]
    return total.astype(jnp.bfloat16)

def reference(slc, row_offset, col_offset, valid):
    row_w = tap_weights(row_offset)
    col_w = tap_weights(col_offset)
    moved = jnp.moveaxis(slc, 1, 0)
    resampled = lax.map(resample_one, (moved, row_w, col_w))
    valid_f = valid.astype(jnp.float32)

    def row_grams(index):
        block = lax.dynamic_slice_in_dim(resampled, index * 4, 4, axis=2)
        samples = block.reshape(DATES, 2, 4, MLRG, 20).transpose(1, 3, 0, 2, 4).reshape(2, MLRG, DATES, 80)
        samples = samples.astype(jnp.float32)
        real_part, imag_part = (samples[0], samples[1])

        def product(left, right):
            return jnp.einsum('mds,mes->mde', left, right, precision=lax.Precision.HIGHEST)
        cross_re = (product(real_part, real_part) + product(imag_part, imag_part)) / 80.0
        cross_im = (product(imag_part, real_part) - product(real_part, imag_part)) / 80.0
        scale = lax.rsqrt(jnp.diagonal(cross_re, axis1=1, axis2=2) + 1e-06)
        mask = lax.dynamic_index_in_dim(valid_f, index, 0, keepdims=False)
        magnitude = jnp.sqrt(cross_re * cross_re + cross_im * cross_im) * scale[:, :, None] * scale[:, None, :]
        gram = (magnitude * (mask[:, :, None] * mask[:, None, :])).astype(jnp.bfloat16)
        pair_list = []
        for step in range(1, PAIRS + 1):
            far = jnp.pad(scale[:, step:], ((0, 0), (0, step)))
            far_mask = jnp.pad(mask[:, step:], ((0, 0), (0, step)))
            real_pair = jnp.pad(jnp.diagonal(cross_re, offset=step, axis1=1, axis2=2), ((0, 0), (0, step)))
            imag_pair = jnp.pad(jnp.diagonal(cross_im, offset=step, axis1=1, axis2=2), ((0, 0), (0, step)))
            both_masks = mask * far_mask
            pair_list.append(jnp.stack([real_pair * scale * far * both_masks, imag_pair * scale * far * both_masks], axis=1))
        return (gram, jnp.stack(pair_list, axis=1))
    coherence, pair_coherence = lax.map(row_grams, jnp.arange(MLAZ).astype(jnp.int32))
    return (coherence, pair_coherence)
```

```python
import functools

import jax
import jax.numpy as jnp
from jax import lax
from jax.experimental import pallas as pl
from jax.experimental.pallas import tpu as pltpu
from jax.sharding import PartitionSpec as P

MESH = pl.DeviceIdType.MESH
PEERS = 32
RANGE = 16
LOOKS = 20
CHUNKS = ((1, 2, 3), (0,), (4,))


def sin_pi(r):
    q = r * r
    total = jnp.full_like(q, 0.000466302805767612)
    for c in (-0.00737043094571435, 0.0821458866111282, -0.599264529320792, 2.55016403987735, -5.16771278004997):
        total = total * q + c
    return r * (total * q + 3.14159265358979)


def sinc(x):
    whole = jnp.round(x)
    odd = whole - 2.0 * jnp.floor(whole * 0.5)
    value = sin_pi(x - whole) * (1.0 - 2.0 * odd)
    zero = x == 0.0
    return jnp.where(zero, 1.0, value / jnp.where(zero, 1.0, x * 3.14159265358979))


def lanczos(x):
    return jnp.where(jnp.abs(x) < 4.0, sinc(x) * sinc(x * 0.25), 0.0)


def iota(shape, dim):
    return lax.broadcasted_iota(jnp.int32, shape, dim)


def band_matrices(row_ref, col_ref, col_band, row_band):
    sub, lane = iota((8, 128), 0), iota((8, 128), 1)
    offset = jnp.zeros((8, 128), jnp.int32)
    for date in range(4):
        offset = jnp.where(sub == date, col_ref[date], offset)
        offset = jnp.where(sub == date + 4, row_ref[date], offset)
    place = jnp.where(lane >= 64, lane - 128, lane)
    tap = jnp.where(sub < 4, -place, place)
    weights = lanczos(offset.astype(jnp.float32) * 0.125 - tap.astype(jnp.float32))
    distance = iota((128, 128), 0) - iota((128, 128), 1)
    inside = jnp.abs(distance) <= 5
    rows = iota((128, 128), 0)
    lines = 4 * (rows % 32) + rows // 32
    line_inside = jnp.abs(lines - iota((128, 128), 1)) <= 5
    for date in range(4):
        line = jnp.broadcast_to(weights[date : date + 1], (8, 128))
        base = pltpu.roll(line, 0, 1, stride=1, stride_axis=0)
        ring = jnp.concatenate([base if b == 0 else pltpu.roll(base, 8 * b, 1) for b in range(16)], axis=0)
        col_band[date, :128] = jnp.where(inside, ring, 0.0).astype(jnp.bfloat16)
        col_band[date, 128:] = jnp.where(inside, 0.0, ring).astype(jnp.bfloat16)
        line = jnp.broadcast_to(weights[date + 4 : date + 5], (8, 128))
        base = pltpu.roll(line, 0, 1, stride=4, stride_axis=0)
        parts = []
        for a in range(4):
            for m in range(0, 32, 8):
                shift = 4 * m + a
                parts.append(base if shift == 0 else pltpu.roll(base, shift, 1))
        ring = jnp.concatenate(parts, axis=0)
        row_band[date] = jnp.where(line_inside, ring, 0.0).astype(jnp.bfloat16)


def resample(windows, slc, low, high, col_band, row_band, stage, send):
    low_lane = iota((128, 128), 1) < 64
    for date in range(4):
        left = []
        for window in windows:
            for part in range(2):
                def block(index):
                    return slc[part, date, :, index * 128 : index * 128 + 128]
                before = low[part, date] if window == 0 else block(window - 1)
                after = high[part, date] if window == 4 else block(window + 1)
                rim = jnp.where(low_lane, after, before)
                left.append(jnp.concatenate([block(window), rim], axis=1))
        left = jnp.concatenate(left, axis=0)
        across = jnp.dot(left, col_band[date], preferred_element_type=jnp.float32).astype(jnp.bfloat16)
        for spot in range(len(windows)):
            first = across[spot * 256 : spot * 256 + 128]
            second = across[spot * 256 + 128 : spot * 256 + 256]
            both = jnp.concatenate([first, second], axis=1)
            lines = jnp.dot(row_band[date], both, preferred_element_type=jnp.float32)
            for part in range(2):
                for a in range(4):
                    stage[spot, pl.ds(a * 8 + part * 4 + date, 32, stride=32), :] = lines[
                        a * 32 : a * 32 + 32, part * 128 : part * 128 + 128
                    ]
    for spot in range(len(windows)):
        send[:, :, spot * 128 : spot * 128 + 128] = (
            stage[spot].astype(jnp.bfloat16).reshape(PEERS, 32, 128)
        )


def gather_rows(spot, window, recv, stack):
    upper = iota((2, 4, 8, 128), 2) < 4
    for group in range(8):
        block = recv[4 * group : 4 * group + 4, :, spot * 128 : spot * 128 + 128]
        block = block.astype(jnp.float32).reshape(2, 2, 4, 8, 128)
        first, second = block[:, 0], block[:, 1]
        real = jnp.where(upper, first, pltpu.roll(second, 4, 2))
        imag = jnp.where(upper, pltpu.roll(first, 4, 2), second)
        for a in range(4):
            lanes = slice(a * 128, a * 128 + 128)
            stack[window, 16 * group : 16 * group + 16, lanes] = (
                real[:, a].reshape(16, 128).astype(jnp.bfloat16)
            )
            stack[window, 128 + 16 * group : 144 + 16 * group, lanes] = (
                imag[:, a].reshape(16, 128).astype(jnp.bfloat16)
            )


def pixel(index, windows, stack, valid, out, pair):
    gram = None
    lane = iota((1, 512), 1) % 128
    for window in windows:
        start = index * LOOKS - window * 128
        mask = jnp.where((lane >= start) & (lane < start + LOOKS), 1.0, 0.0).astype(jnp.bfloat16)
        rows = stack[window]
        term = lax.dot_general(
            rows * mask, rows, (((1,), (1,)), ((), ())), preferred_element_type=jnp.float32
        )
        gram = term if gram is None else gram + term
    real = gram[:128, :128] + gram[128:, 128:]
    imag = gram[128:, :128] - gram[:128, 128:]
    sub, col = iota((8, 128), 0), iota((8, 128), 1)
    block = (sub - col) >> 3
    step = (sub - col) & 7
    near_re = jnp.zeros((8, 128), jnp.float32)
    near_im = jnp.zeros((8, 128), jnp.float32)
    for b in range(16):
        near_re = jnp.where(block == -b, real[8 * b : 8 * b + 8], near_re)
        near_im = jnp.where(block == -b, imag[8 * b : 8 * b + 8], near_im)

    def diagonal(near, k):
        return jnp.sum(jnp.where(step == k, near, 0.0), axis=0, keepdims=True)

    power = diagonal(near_re, 0) + 8e-5
    mask = valid[pl.ds(index, 1), :].astype(jnp.float32)
    scale = lax.rsqrt(power) * mask
    square = scale * scale
    eye = iota((128, 128), 0) == iota((128, 128), 1)
    down = jnp.sum(jnp.where(eye, jnp.broadcast_to(square, (128, 128)), 0.0), axis=1, keepdims=True)
    value = (real * real + imag * imag) * square * down
    out[index] = jnp.where(value > 0.0, value * lax.rsqrt(value), 0.0).astype(jnp.bfloat16)
    pieces = []
    for k in range(1, 5):
        both = scale * pltpu.roll(scale, 128 - k, 1)
        pieces.append(diagonal(near_re, k) * both)
        pieces.append(-diagonal(near_im, k) * both)
    pair[index] = jnp.concatenate(pieces, axis=0)


def kernel(
    row_ref, col_ref, slc, valid, coherence, pair,
    low, high, col_band, row_band, stage, send_a, send_b, send_c, recv_a, recv_b, recv_c, stack, out,
    halo_sem, send_sem, recv_sem, own_sem, out_sem,
):
    date = lax.axis_index("date")
    spot = lax.axis_index("range")
    right = lax.rem(spot + 1, RANGE)
    left = lax.rem(spot + RANGE - 1, RANGE)
    barrier = pltpu.get_barrier_semaphore()
    for to in (left, right):
        pl.semaphore_signal(barrier, inc=1, device_id={"range": to}, device_id_type=MESH)

    def greet(step, carry):
        pl.semaphore_signal(
            barrier, inc=1, device_id={"date": lax.rem(date + step, PEERS)}, device_id_type=MESH
        )
        return carry

    lax.fori_loop(1, PEERS, greet, 0)
    band_matrices(row_ref, col_ref, col_band, row_band)
    sends, recvs = (send_a, send_b, send_c), (recv_a, recv_b, recv_c)
    resample(CHUNKS[0], slc, low, high, col_band, row_band, stage, send_a)
    pl.semaphore_wait(barrier, PEERS + 1)

    def launch(chunk):
        def one(step, carry):
            to = lax.rem(date + step, PEERS)
            pltpu.make_async_remote_copy(
                src_ref=sends[chunk].at[to],
                dst_ref=recvs[chunk].at[date],
                send_sem=send_sem.at[chunk],
                recv_sem=recv_sem.at[chunk],
                device_id={"date": to},
                device_id_type=MESH,
            ).start()
            return carry

        lax.fori_loop(1, PEERS, one, 0)
        pltpu.make_async_copy(sends[chunk].at[date], recvs[chunk].at[date], own_sem.at[chunk]).start()

    def landed(chunk):
        pltpu.make_async_copy(
            sends[chunk].at[date], recvs[chunk].at[date], own_sem.at[chunk]
        ).wait()
        some = recvs[chunk].at[pl.ds(0, PEERS - 1)]
        pltpu.make_async_copy(some, some, recv_sem.at[chunk]).wait()

    to_right = pltpu.make_async_remote_copy(
        src_ref=slc.at[:, :, :, pl.ds(512, 128)], dst_ref=low,
        send_sem=halo_sem.at[0], recv_sem=halo_sem.at[1],
        device_id={"range": right}, device_id_type=MESH,
    )
    to_left = pltpu.make_async_remote_copy(
        src_ref=slc.at[:, :, :, pl.ds(0, 128)], dst_ref=high,
        send_sem=halo_sem.at[2], recv_sem=halo_sem.at[3],
        device_id={"range": left}, device_id_type=MESH,
    )
    to_right.start()
    to_left.start()
    launch(0)
    to_right.wait()
    to_left.wait()

    @pl.when(spot == 0)
    def _():
        low[...] = jnp.zeros_like(low)

    @pl.when(spot == RANGE - 1)
    def _():
        high[...] = jnp.zeros_like(high)

    for chunk in (1, 2):
        resample(CHUNKS[chunk], slc, low, high, col_band, row_band, stage, sends[chunk])
        launch(chunk)

    def pixels(first, last, window):
        def one(index, carry):
            pixel(index, (window,), stack, valid, out, pair)
            return carry

        lax.fori_loop(first, last, one, 0)

    def store(first, last, slot):
        return pltpu.make_async_copy(
            out.at[pl.ds(first, last - first)], coherence.at[pl.ds(first, last - first)], out_sem.at[slot]
        )

    landed(0)
    for place, window in enumerate(CHUNKS[0]):
        gather_rows(place, window, recv_a, stack)
    pixels(7, 12, 1)
    pixel(12, (1, 2), stack, valid, out, pair)
    pixels(13, 19, 2)
    pixel(19, (2, 3), stack, valid, out, pair)
    pixels(20, 25, 3)
    store(7, 25, 0).start()
    landed(1)
    gather_rows(0, 0, recv_b, stack)
    pixels(0, 6, 0)
    pixel(6, (0, 1), stack, valid, out, pair)
    store(0, 7, 1).start()
    landed(2)
    gather_rows(0, 4, recv_c, stack)
    pixel(25, (3, 4), stack, valid, out, pair)
    pixels(26, 32, 4)
    store(25, 32, 2).start()
    for chunk in range(3):
        some = sends[chunk].at[pl.ds(0, PEERS - 1)]
        pltpu.make_async_copy(some, some, send_sem.at[chunk]).wait()
    store(7, 25, 0).wait()
    store(0, 7, 1).wait()
    store(25, 32, 2).wait()


def on_device(slc, row_offset, col_offset, valid):
    bf16 = jnp.bfloat16
    vmem = pl.BlockSpec(memory_space=pltpu.VMEM)
    smem = pl.BlockSpec(memory_space=pltpu.SMEM)
    blocks = [pltpu.VMEM((PEERS, 32, 128 * len(chunk)), bf16) for chunk in CHUNKS]
    coherence, pair = pl.pallas_call(
        kernel,
        out_shape=(
            jax.ShapeDtypeStruct((32, 128, 128), bf16),
            jax.ShapeDtypeStruct((32, 8, 128), jnp.float32),
        ),
        in_specs=[smem, smem, vmem, vmem],
        out_specs=(pl.BlockSpec(memory_space=pl.ANY), vmem),
        scratch_shapes=[
            pltpu.VMEM((2, 4, 128, 128), bf16),
            pltpu.VMEM((2, 4, 128, 128), bf16),
            pltpu.VMEM((4, 256, 128), bf16),
            pltpu.VMEM((4, 128, 128), bf16),
            pltpu.VMEM((3, 1024, 128), jnp.float32),
            *blocks,
            *blocks,
            pltpu.VMEM((5, 256, 512), bf16),
            pltpu.VMEM((32, 128, 128), bf16),
            pltpu.SemaphoreType.DMA((4,)),
            pltpu.SemaphoreType.DMA((3,)),
            pltpu.SemaphoreType.DMA((3,)),
            pltpu.SemaphoreType.DMA((3,)),
            pltpu.SemaphoreType.DMA((3,)),
        ],
        compiler_params=pltpu.CompilerParams(
            collective_id=0, has_side_effects=True, vmem_limit_bytes=48 << 20
        ),
    )(row_offset, col_offset, slc, valid[0])
    return coherence[None], pair.reshape(1, 32, 4, 2, 128)


def solution(mesh):
    in_specs = (P(None, "date", None, "range"), P("date"), P("date"), P("date", "range", None))
    out_specs = (P("date", "range", None, None), P("date", "range", None, None, None))
    return jax.shard_map(
        on_device, mesh=mesh, in_specs=in_specs, out_specs=out_specs, check_vma=False
    )
```

```python
import functools

import jax
import jax.numpy as jnp
from jax import lax
from jax.experimental import pallas as pl
from jax.experimental.pallas import tpu as pltpu
from jax.sharding import PartitionSpec as P

MESH = pl.DeviceIdType.MESH
PEERS = 32
RANGE = 16
LOOKS = 20
CHUNKS = ((1, 2, 3), (0, 4))


def sin_pi(r):
    q = r * r
    total = jnp.full_like(q, 0.000466302805767612)
    for c in (-0.00737043094571435, 0.0821458866111282, -0.599264529320792, 2.55016403987735, -5.16771278004997):
        total = total * q + c
    return r * (total * q + 3.14159265358979)


def sinc(x):
    whole = jnp.round(x)
    odd = whole - 2.0 * jnp.floor(whole * 0.5)
    value = sin_pi(x - whole) * (1.0 - 2.0 * odd)
    zero = x == 0.0
    return jnp.where(zero, 1.0, value / jnp.where(zero, 1.0, x * 3.14159265358979))


def lanczos(x):
    return jnp.where(jnp.abs(x) < 4.0, sinc(x) * sinc(x * 0.25), 0.0)


def iota(shape, dim):
    return lax.broadcasted_iota(jnp.int32, shape, dim)


def band_matrices(row_ref, col_ref, col_band, row_band):
    sub, lane = iota((8, 128), 0), iota((8, 128), 1)
    offset = jnp.zeros((8, 128), jnp.int32)
    for date in range(4):
        offset = jnp.where(sub == date, col_ref[date], offset)
        offset = jnp.where(sub == date + 4, row_ref[date], offset)
    place = jnp.where(lane >= 64, lane - 128, lane)
    tap = jnp.where(sub < 4, -place, place)
    weights = lanczos(offset.astype(jnp.float32) * 0.125 - tap.astype(jnp.float32))
    distance = iota((128, 128), 0) - iota((128, 128), 1)
    inside = jnp.abs(distance) <= 5
    rows = iota((128, 128), 0)
    lines = 4 * (rows % 32) + rows // 32
    line_inside = jnp.abs(lines - iota((128, 128), 1)) <= 5
    for date in range(4):
        line = jnp.broadcast_to(weights[date : date + 1], (8, 128))
        base = pltpu.roll(line, 0, 1, stride=1, stride_axis=0)
        ring = jnp.concatenate([base if b == 0 else pltpu.roll(base, 8 * b, 1) for b in range(16)], axis=0)
        col_band[date, :128] = jnp.where(inside, ring, 0.0).astype(jnp.bfloat16)
        col_band[date, 128:] = jnp.where(inside, 0.0, ring).astype(jnp.bfloat16)
        line = jnp.broadcast_to(weights[date + 4 : date + 5], (8, 128))
        base = pltpu.roll(line, 0, 1, stride=4, stride_axis=0)
        parts = []
        for a in range(4):
            for m in range(0, 32, 8):
                shift = 4 * m + a
                parts.append(base if shift == 0 else pltpu.roll(base, shift, 1))
        ring = jnp.concatenate(parts, axis=0)
        row_band[date] = jnp.where(line_inside, ring, 0.0).astype(jnp.bfloat16)


def resample(windows, slc, low, high, col_band, row_band, stage, send):
    low_lane = iota((128, 128), 1) < 64
    for date in range(4):
        left = []
        for window in windows:
            for part in range(2):
                def block(index):
                    return slc[part, date, :, index * 128 : index * 128 + 128]
                before = low[part, date] if window == 0 else block(window - 1)
                after = high[part, date] if window == 4 else block(window + 1)
                rim = jnp.where(low_lane, after, before)
                left.append(jnp.concatenate([block(window), rim], axis=1))
        left = jnp.concatenate(left, axis=0)
        across = jnp.dot(left, col_band[date], preferred_element_type=jnp.float32).astype(jnp.bfloat16)
        for spot in range(len(windows)):
            first = across[spot * 256 : spot * 256 + 128]
            second = across[spot * 256 + 128 : spot * 256 + 256]
            both = jnp.concatenate([first, second], axis=1)
            lines = jnp.dot(row_band[date], both, preferred_element_type=jnp.float32)
            for part in range(2):
                for a in range(4):
                    stage[spot, pl.ds(a * 8 + part * 4 + date, 32, stride=32), :] = lines[
                        a * 32 : a * 32 + 32, part * 128 : part * 128 + 128
                    ]
    for spot in range(len(windows)):
        send[:, :, spot * 128 : spot * 128 + 128] = (
            stage[spot].astype(jnp.bfloat16).reshape(PEERS, 32, 128)
        )


def gather_rows(spot, window, recv, stack):
    upper = iota((2, 4, 8, 128), 2) < 4
    for group in range(8):
        block = recv[4 * group : 4 * group + 4, :, spot * 128 : spot * 128 + 128]
        block = block.astype(jnp.float32).reshape(2, 2, 4, 8, 128)
        first, second = block[:, 0], block[:, 1]
        real = jnp.where(upper, first, pltpu.roll(second, 4, 2))
        imag = jnp.where(upper, pltpu.roll(first, 4, 2), second)
        for a in range(4):
            lanes = slice(a * 128, a * 128 + 128)
            stack[window, 16 * group : 16 * group + 16, lanes] = (
                real[:, a].reshape(16, 128).astype(jnp.bfloat16)
            )
            stack[window, 128 + 16 * group : 144 + 16 * group, lanes] = (
                imag[:, a].reshape(16, 128).astype(jnp.bfloat16)
            )


def pixel(index, windows, stack, valid, out, pair):
    gram = None
    lane = iota((1, 512), 1) % 128
    for window in windows:
        start = index * LOOKS - window * 128
        mask = jnp.where((lane >= start) & (lane < start + LOOKS), 1.0, 0.0).astype(jnp.bfloat16)
        rows = stack[window]
        term = lax.dot_general(
            rows * mask, rows, (((1,), (1,)), ((), ())), preferred_element_type=jnp.float32
        )
        gram = term if gram is None else gram + term
    real = gram[:128, :128] + gram[128:, 128:]
    imag = gram[128:, :128] - gram[:128, 128:]
    sub, col = iota((8, 128), 0), iota((8, 128), 1)
    block = (sub - col) >> 3
    step = (sub - col) & 7
    near_re = jnp.zeros((8, 128), jnp.float32)
    near_im = jnp.zeros((8, 128), jnp.float32)
    for b in range(16):
        near_re = jnp.where(block == -b, real[8 * b : 8 * b + 8], near_re)
        near_im = jnp.where(block == -b, imag[8 * b : 8 * b + 8], near_im)

    def diagonal(near, k):
        return jnp.sum(jnp.where(step == k, near, 0.0), axis=0, keepdims=True)

    power = diagonal(near_re, 0) + 8e-5
    mask = valid[pl.ds(index, 1), :].astype(jnp.float32)
    scale = lax.rsqrt(power) * mask
    square = scale * scale
    eye = iota((128, 128), 0) == iota((128, 128), 1)
    down = jnp.sum(jnp.where(eye, jnp.broadcast_to(square, (128, 128)), 0.0), axis=1, keepdims=True)
    value = (real * real + imag * imag) * square * down
    out[index] = jnp.where(value > 0.0, value * lax.rsqrt(value), 0.0).astype(jnp.bfloat16)
    pieces = []
    for k in range(1, 5):
        both = scale * pltpu.roll(scale, 128 - k, 1)
        pieces.append(diagonal(near_re, k) * both)
        pieces.append(-diagonal(near_im, k) * both)
    pair[index] = jnp.concatenate(pieces, axis=0).reshape(4, 2, 128)


def kernel(
    row_in, col_in, slc_in, valid_in, out, pair,
    row_ref, col_ref, slc, valid, in_sem,
    low, high, col_band, row_band, stage, send_a, send_b, recv_a, recv_b, stack,
    halo_sem, send_sem, recv_sem, own_sem,
):
    date = lax.axis_index("date")
    spot = lax.axis_index("range")
    right = lax.rem(spot + 1, RANGE)
    left = lax.rem(spot + RANGE - 1, RANGE)
    barrier = pltpu.get_barrier_semaphore()
    for to in (left, right):
        pl.semaphore_signal(barrier, inc=1, device_id={"range": to}, device_id_type=MESH)

    def greet(step, carry):
        pl.semaphore_signal(
            barrier, inc=1, device_id={"date": lax.rem(date + step, PEERS)}, device_id_type=MESH
        )
        return carry

    lax.fori_loop(1, PEERS, greet, 0)
    loads = [
        pltpu.make_async_copy(source, target, in_sem.at[slot])
        for slot, (source, target) in enumerate(
            ((row_in, row_ref), (col_in, col_ref), (slc_in, slc), (valid_in, valid))
        )
    ]
    for load in loads:
        load.start()
    loads[0].wait()
    loads[1].wait()
    band_matrices(row_ref, col_ref, col_band, row_band)
    loads[2].wait()
    loads[3].wait()
    sends, recvs = (send_a, send_b), (recv_a, recv_b)
    resample(CHUNKS[0], slc, low, high, col_band, row_band, stage, send_a)
    pl.semaphore_wait(barrier, PEERS + 1)

    def launch(chunk):
        def one(step, carry):
            pair_at = step // 4
            to = (pair_at // 2 + 4 * (pair_at % 2)) * 4 + lax.rem(date + step, 4)

            @pl.when(to != date)
            def _():
                pltpu.make_async_remote_copy(
                    src_ref=sends[chunk].at[to],
                    dst_ref=recvs[chunk].at[date],
                    send_sem=send_sem.at[chunk],
                    recv_sem=recv_sem.at[chunk],
                    device_id={"date": to},
                    device_id_type=MESH,
                ).start()

            return carry

        lax.fori_loop(0, PEERS, one, 0)
        pltpu.make_async_copy(sends[chunk].at[date], recvs[chunk].at[date], own_sem.at[chunk]).start()

    def landed(chunk):
        pltpu.make_async_copy(
            sends[chunk].at[date], recvs[chunk].at[date], own_sem.at[chunk]
        ).wait()
        some = recvs[chunk].at[pl.ds(0, PEERS - 1)]
        pltpu.make_async_copy(some, some, recv_sem.at[chunk]).wait()

    to_right = pltpu.make_async_remote_copy(
        src_ref=slc.at[:, :, :, pl.ds(512, 128)], dst_ref=low,
        send_sem=halo_sem.at[0], recv_sem=halo_sem.at[1],
        device_id={"range": right}, device_id_type=MESH,
    )
    to_left = pltpu.make_async_remote_copy(
        src_ref=slc.at[:, :, :, pl.ds(0, 128)], dst_ref=high,
        send_sem=halo_sem.at[2], recv_sem=halo_sem.at[3],
        device_id={"range": left}, device_id_type=MESH,
    )
    to_right.start()
    to_left.start()
    launch(0)
    to_right.wait()
    to_left.wait()

    @pl.when(spot == 0)
    def _():
        low[...] = jnp.zeros_like(low)

    @pl.when(spot == RANGE - 1)
    def _():
        high[...] = jnp.zeros_like(high)

    resample(CHUNKS[1], slc, low, high, col_band, row_band, stage, send_b)
    launch(1)

    def pixels(first, last, window):
        def one(index, carry):
            pixel(index, (window,), stack, valid, out, pair)
            return carry

        for index in range(first, last):
            one(index, 0)

    landed(0)
    for place, window in enumerate(CHUNKS[0]):
        gather_rows(place, window, recv_a, stack)
    pixels(7, 12, 1)
    pixel(12, (1, 2), stack, valid, out, pair)
    pixels(13, 19, 2)
    pixel(19, (2, 3), stack, valid, out, pair)
    pixels(20, 25, 3)
    landed(1)
    gather_rows(0, 0, recv_b, stack)
    gather_rows(1, 4, recv_b, stack)
    pixels(0, 6, 0)
    pixel(6, (0, 1), stack, valid, out, pair)
    pixel(25, (3, 4), stack, valid, out, pair)
    pixels(26, 32, 4)
    for chunk in range(2):
        some = sends[chunk].at[pl.ds(0, PEERS - 1)]
        pltpu.make_async_copy(some, some, send_sem.at[chunk]).wait()


def hand_over(coherence, pair, coherence_out, pair_out, sem):
    copies = []
    for part in range(4):
        rows = pl.ds(part * 8, 8)
        copies.append(pltpu.make_async_copy(coherence.at[rows], coherence_out.at[rows], sem.at[part]))
    copies.append(pltpu.make_async_copy(pair, pair_out, sem.at[4]))
    for copy in copies:
        copy.start()
    for copy in copies:
        copy.wait()


def on_device(slc, row_offset, col_offset, valid):
    bf16 = jnp.bfloat16
    vmem = pl.BlockSpec(memory_space=pltpu.VMEM)
    hbm = pl.BlockSpec(memory_space=pltpu.HBM)
    blocks = [pltpu.VMEM((PEERS, 32, 128 * len(chunk)), bf16) for chunk in CHUNKS]
    coherence, pair = pl.pallas_call(
        kernel,
        out_shape=(
            pltpu.VMEM((32, 128, 128), bf16),
            pltpu.VMEM((32, 4, 2, 128), jnp.float32),
        ),
        in_specs=[hbm, hbm, hbm, hbm],
        out_specs=(vmem, vmem),
        scratch_shapes=[
            pltpu.SMEM((4,), jnp.int32),
            pltpu.SMEM((4,), jnp.int32),
            pltpu.VMEM((2, 4, 128, 640), bf16),
            pltpu.VMEM((32, 128), jnp.int32),
            pltpu.SemaphoreType.DMA((4,)),
            pltpu.VMEM((2, 4, 128, 128), bf16),
            pltpu.VMEM((2, 4, 128, 128), bf16),
            pltpu.VMEM((4, 256, 128), bf16),
            pltpu.VMEM((4, 128, 128), bf16),
            pltpu.VMEM((3, 1024, 128), jnp.float32),
            *blocks,
            *blocks,
            pltpu.VMEM((5, 256, 512), bf16),
            pltpu.SemaphoreType.DMA((4,)),
            pltpu.SemaphoreType.DMA((2,)),
            pltpu.SemaphoreType.DMA((2,)),
            pltpu.SemaphoreType.DMA((2,)),
        ],
        compiler_params=pltpu.CompilerParams(
            collective_id=0, has_side_effects=True, vmem_limit_bytes=60 << 20
        ),
    )(row_offset, col_offset, slc, valid[0])
    hbm = pl.BlockSpec(memory_space=pltpu.HBM)
    coherence, pair = pl.pallas_call(
        hand_over,
        out_shape=(
            jax.ShapeDtypeStruct((32, 128, 128), bf16),
            jax.ShapeDtypeStruct((32, 4, 2, 128), jnp.float32),
        ),
        in_specs=[vmem, vmem],
        out_specs=(hbm, hbm),
        scratch_shapes=[pltpu.SemaphoreType.DMA((5,))],
        compiler_params=pltpu.CompilerParams(vmem_limit_bytes=4 << 20),
    )(coherence, pair)
    return coherence[None], pair[None]


def solution(mesh):
    in_specs = (P(None, "date", None, "range"), P("date"), P("date"), P("date", "range", None))
    out_specs = (P("date", "range", None, None), P("date", "range", None, None, None))
    return jax.shard_map(
        on_device, mesh=mesh, in_specs=in_specs, out_specs=out_specs, check_vma=False
    )
```

```python
import functools

import jax
import jax.numpy as jnp
from jax import lax
from jax.experimental import pallas as pl
from jax.experimental.pallas import tpu as pltpu
from jax.sharding import PartitionSpec as P

MESH = pl.DeviceIdType.MESH
PEERS = 32
RANGE = 16
LOOKS = 20
CHUNKS = ((1, 2, 3), (0, 4))


def sin_pi(r):
    q = r * r
    total = jnp.full_like(q, 0.000466302805767612)
    for c in (-0.00737043094571435, 0.0821458866111282, -0.599264529320792, 2.55016403987735, -5.16771278004997):
        total = total * q + c
    return r * (total * q + 3.14159265358979)


def sinc(x):
    whole = jnp.round(x)
    odd = whole - 2.0 * jnp.floor(whole * 0.5)
    value = sin_pi(x - whole) * (1.0 - 2.0 * odd)
    zero = x == 0.0
    return jnp.where(zero, 1.0, value / jnp.where(zero, 1.0, x * 3.14159265358979))


def lanczos(x):
    return jnp.where(jnp.abs(x) < 4.0, sinc(x) * sinc(x * 0.25), 0.0)


def iota(shape, dim):
    return lax.broadcasted_iota(jnp.int32, shape, dim)


def band_matrices(row_ref, col_ref, col_band, row_band):
    sub, lane = iota((8, 128), 0), iota((8, 128), 1)
    offset = jnp.zeros((8, 128), jnp.int32)
    for date in range(4):
        offset = jnp.where(sub == date, col_ref[date], offset)
        offset = jnp.where(sub == date + 4, row_ref[date], offset)
    place = jnp.where(lane >= 64, lane - 128, lane)
    tap = jnp.where(sub < 4, -place, place)
    weights = lanczos(offset.astype(jnp.float32) * 0.125 - tap.astype(jnp.float32))
    distance = iota((128, 128), 0) - iota((128, 128), 1)
    inside = jnp.abs(distance) <= 5
    first = sub < 4
    reach = [jnp.abs(lane - 4 * m - sub % 4) <= 5 for m in range(32)]
    for date in range(4):
        line = jnp.broadcast_to(weights[date : date + 1], (8, 128))
        base = pltpu.roll(line, 0, 1, stride=1, stride_axis=0)
        ring = jnp.concatenate([base if b == 0 else pltpu.roll(base, 8 * b, 1) for b in range(16)], axis=0)
        col_band[date, :128] = jnp.where(inside, ring, 0.0).astype(jnp.bfloat16)
        col_band[date, 128:] = jnp.where(inside, 0.0, ring).astype(jnp.bfloat16)
        line = jnp.broadcast_to(weights[date + 4 : date + 5], (8, 128))
        base = pltpu.roll(line, 0, 1, stride=1, stride_axis=0)
        base = jnp.where(first, base, pltpu.roll(base, 124, 1))
        real, imag = [], []
        for m in range(32):
            ring = base if m == 0 else pltpu.roll(base, 4 * m, 1)
            real.append(jnp.where(reach[m] & first, ring, 0.0))
            imag.append(jnp.where(reach[m] & ~first, ring, 0.0))
        row_band[date, :, :128] = jnp.concatenate(real, axis=0).astype(jnp.bfloat16)
        row_band[date, :, 128:] = jnp.concatenate(imag, axis=0).astype(jnp.bfloat16)


def resample(windows, slc, low, high, col_band, row_band, send):
    low_lane = iota((128, 128), 1) < 64
    count = len(windows)
    for pair in range(2):
        results = []
        for date in (2 * pair, 2 * pair + 1):
            left = []
            for window in windows:
                for part in range(2):
                    def block(index):
                        return slc[part, date, :, index * 128 : index * 128 + 128]
                    before = low[part, date] if window == 0 else block(window - 1)
                    after = high[part, date] if window == 4 else block(window + 1)
                    rim = jnp.where(low_lane, after, before)
                    left.append(jnp.concatenate([block(window), rim], axis=1))
            left = jnp.concatenate(left, axis=0)
            across = jnp.dot(left, col_band[date], preferred_element_type=jnp.float32).astype(jnp.bfloat16)
            across = jnp.concatenate([across[i * 256 : i * 256 + 256] for i in range(count)], axis=1)
            lines = jnp.dot(row_band[date], across, preferred_element_type=jnp.float32)
            results.append(lines.reshape(PEERS, 8, 128 * count))
        both = jnp.concatenate(results, axis=1)
        send[:, 16 * pair : 16 * pair + 16, :] = both.astype(jnp.bfloat16)


def gather_rows(windows, recv, swap, stack):
    lanes = 128 * len(windows)
    low = iota((64, 128), 1) < 64
    for group in range(4):
        block = recv[8 * group : 8 * group + 8].reshape(256, lanes)
        rows = jnp.dot(swap[...], block, preferred_element_type=jnp.float32)
        for place, window in enumerate(windows):
            for pair in range(2):
                first = rows[128 * pair : 128 * pair + 64, place * 128 : place * 128 + 128]
                second = rows[128 * pair + 64 : 128 * pair + 128, place * 128 : place * 128 + 128]
                second = pltpu.roll(second, 64, 1)
                for half in range(2):
                    mixed = jnp.where(low, second, first) if half else jnp.where(low, first, second)
                    mixed = mixed.astype(jnp.bfloat16)
                    for part in range(2):
                        to = part * 128 + group * 32
                        stack[2 * window + half, to : to + 32, pair * 128 : pair * 128 + 128] = mixed[
                            part * 32 : part * 32 + 32
                        ]


def pixel(index, stack, valid, out, pair):
    gram = None
    lane = iota((1, 256), 1) % 64
    for half in range(index * LOOKS // 64, (index * LOOKS + LOOKS - 1) // 64 + 1):
        start = index * LOOKS - half * 64
        mask = jnp.where((lane >= start) & (lane < start + LOOKS), 1.0, 0.0).astype(jnp.bfloat16)
        rows = stack[half]
        term = lax.dot_general(
            rows * mask, rows, (((1,), (1,)), ((), ())), preferred_element_type=jnp.float32
        )
        gram = term if gram is None else gram + term
    real = gram[:128, :128] + gram[128:, 128:]
    imag = gram[128:, :128] - gram[:128, 128:]
    sub, col = iota((8, 128), 0), iota((8, 128), 1)
    block = (sub - col) >> 3
    step = (sub - col) & 7
    near_re = jnp.zeros((8, 128), jnp.float32)
    near_im = jnp.zeros((8, 128), jnp.float32)
    for b in range(16):
        near_re = jnp.where(block == -b, real[8 * b : 8 * b + 8], near_re)
        near_im = jnp.where(block == -b, imag[8 * b : 8 * b + 8], near_im)

    def diagonal(near, k):
        return jnp.sum(jnp.where(step == k, near, 0.0), axis=0, keepdims=True)

    power = diagonal(near_re, 0) + 8e-5
    mask = valid[pl.ds(index, 1), :].astype(jnp.float32)
    scale = lax.rsqrt(power) * mask
    square = scale * scale
    eye = iota((128, 128), 0) == iota((128, 128), 1)
    down = jnp.sum(jnp.where(eye, jnp.broadcast_to(square, (128, 128)), 0.0), axis=1, keepdims=True)
    value = (real * real + imag * imag) * square * down
    out[index] = jnp.where(value > 0.0, value * lax.rsqrt(value), 0.0).astype(jnp.bfloat16)
    pieces = []
    for k in range(1, 5):
        both = scale * pltpu.roll(scale, 128 - k, 1)
        pieces.append(diagonal(near_re, k) * both)
        pieces.append(-diagonal(near_im, k) * both)
    pair[index] = jnp.concatenate(pieces, axis=0).reshape(4, 2, 128)


def kernel(
    row_in, col_in, slc_in, valid_in, out, pair,
    row_ref, col_ref, slc, valid, in_sem,
    low, high, col_band, row_band, swap, send_a, send_b, recv_a, recv_b, stack,
    halo_sem, send_sem, recv_sem, own_sem,
):
    date = lax.axis_index("date")
    spot = lax.axis_index("range")
    right = lax.rem(spot + 1, RANGE)
    left = lax.rem(spot + RANGE - 1, RANGE)
    barrier = pltpu.get_barrier_semaphore()
    for to in (left, right):
        pl.semaphore_signal(barrier, inc=1, device_id={"range": to}, device_id_type=MESH)

    def greet(step, carry):
        pl.semaphore_signal(
            barrier, inc=1, device_id={"date": lax.rem(date + step, PEERS)}, device_id_type=MESH
        )
        return carry

    lax.fori_loop(1, PEERS, greet, 0)
    loads = [
        pltpu.make_async_copy(source, target, in_sem.at[slot])
        for slot, (source, target) in enumerate(
            ((row_in, row_ref), (col_in, col_ref), (slc_in, slc), (valid_in, valid))
        )
    ]
    for load in loads:
        load.start()
    loads[0].wait()
    loads[1].wait()
    band_matrices(row_ref, col_ref, col_band, row_band)
    loads[2].wait()
    loads[3].wait()
    sends, recvs = (send_a, send_b), (recv_a, recv_b)
    resample(CHUNKS[0], slc, low, high, col_band, row_band, send_a)
    pl.semaphore_wait(barrier, PEERS + 1)

    def launch(chunk):
        for z in (0, 1, 4, 2, 5, 3, 6, 7):

            def one(step, carry):
                to = z * 4 + (step ^ (step >> 1))

                @pl.when(to != date)
                def _():
                    pltpu.make_async_remote_copy(
                        src_ref=sends[chunk].at[to],
                        dst_ref=recvs[chunk].at[date],
                        send_sem=send_sem.at[chunk],
                        recv_sem=recv_sem.at[chunk],
                        device_id={"date": to},
                        device_id_type=MESH,
                    ).start()

                return carry

            lax.fori_loop(0, 4, one, 0)
        pltpu.make_async_copy(sends[chunk].at[date], recvs[chunk].at[date], own_sem.at[chunk]).start()

    def landed(chunk):
        pltpu.make_async_copy(
            sends[chunk].at[date], recvs[chunk].at[date], own_sem.at[chunk]
        ).wait()
        some = recvs[chunk].at[pl.ds(0, PEERS - 1)]
        pltpu.make_async_copy(some, some, recv_sem.at[chunk]).wait()

    to_right = pltpu.make_async_remote_copy(
        src_ref=slc.at[:, :, :, pl.ds(512, 128)], dst_ref=low,
        send_sem=halo_sem.at[0], recv_sem=halo_sem.at[1],
        device_id={"range": right}, device_id_type=MESH,
    )
    to_left = pltpu.make_async_remote_copy(
        src_ref=slc.at[:, :, :, pl.ds(0, 128)], dst_ref=high,
        send_sem=halo_sem.at[2], recv_sem=halo_sem.at[3],
        device_id={"range": left}, device_id_type=MESH,
    )
    to_right.start()
    to_left.start()
    launch(0)
    to_right.wait()
    to_left.wait()

    @pl.when(spot == 0)
    def _():
        low[...] = jnp.zeros_like(low)

    @pl.when(spot == RANGE - 1)
    def _():
        high[...] = jnp.zeros_like(high)

    resample(CHUNKS[1], slc, low, high, col_band, row_band, send_b)
    launch(1)

    def pixels(first, last):
        for index in range(first, last):
            pixel(index, stack, valid, out, pair)

    to_row, from_row = iota((256, 256), 0), iota((256, 256), 1)
    source = (to_row % 32) * 8 + (to_row // 32) % 2 * 4 + to_row // 64
    swap[...] = jnp.where(from_row == source, 1.0, 0.0).astype(jnp.bfloat16)
    landed(0)
    gather_rows(CHUNKS[0], recv_a, swap, stack)
    pixels(7, 25)
    landed(1)
    gather_rows(CHUNKS[1], recv_b, swap, stack)
    pixels(0, 7)
    pixels(25, 32)
    for chunk in range(2):
        some = sends[chunk].at[pl.ds(0, PEERS - 1)]
        pltpu.make_async_copy(some, some, send_sem.at[chunk]).wait()


def hand_over(coherence, pair, coherence_out, pair_out, sem):
    copies = []
    for part in range(4):
        rows = pl.ds(part * 8, 8)
        copies.append(pltpu.make_async_copy(coherence.at[rows], coherence_out.at[rows], sem.at[part]))
    copies.append(pltpu.make_async_copy(pair, pair_out, sem.at[4]))
    for copy in copies:
        copy.start()
    for copy in copies:
        copy.wait()


def on_device(slc, row_offset, col_offset, valid):
    bf16 = jnp.bfloat16
    vmem = pl.BlockSpec(memory_space=pltpu.VMEM)
    hbm = pl.BlockSpec(memory_space=pltpu.HBM)
    blocks = [pltpu.VMEM((PEERS, 32, 128 * len(chunk)), bf16) for chunk in CHUNKS]
    coherence, pair = pl.pallas_call(
        kernel,
        out_shape=(
            pltpu.VMEM((32, 128, 128), bf16),
            pltpu.VMEM((32, 4, 2, 128), jnp.float32),
        ),
        in_specs=[hbm, hbm, hbm, hbm],
        out_specs=(vmem, vmem),
        scratch_shapes=[
            pltpu.SMEM((4,), jnp.int32),
            pltpu.SMEM((4,), jnp.int32),
            pltpu.VMEM((2, 4, 128, 640), bf16),
            pltpu.VMEM((32, 128), jnp.int32),
            pltpu.SemaphoreType.DMA((4,)),
            pltpu.VMEM((2, 4, 128, 128), bf16),
            pltpu.VMEM((2, 4, 128, 128), bf16),
            pltpu.VMEM((4, 256, 128), bf16),
            pltpu.VMEM((4, 256, 256), bf16),
            pltpu.VMEM((256, 256), bf16),
            *blocks,
            *blocks,
            pltpu.VMEM((10, 256, 256), bf16),
            pltpu.SemaphoreType.DMA((4,)),
            pltpu.SemaphoreType.DMA((2,)),
            pltpu.SemaphoreType.DMA((2,)),
            pltpu.SemaphoreType.DMA((2,)),
        ],
        compiler_params=pltpu.CompilerParams(
            collective_id=0, has_side_effects=True, vmem_limit_bytes=60 << 20
        ),
    )(row_offset, col_offset, slc, valid[0])
    hbm = pl.BlockSpec(memory_space=pltpu.HBM)
    coherence, pair = pl.pallas_call(
        hand_over,
        out_shape=(
            jax.ShapeDtypeStruct((32, 128, 128), bf16),
            jax.ShapeDtypeStruct((32, 4, 2, 128), jnp.float32),
        ),
        in_specs=[vmem, vmem],
        out_specs=(hbm, hbm),
        scratch_shapes=[pltpu.SemaphoreType.DMA((5,))],
        compiler_params=pltpu.CompilerParams(vmem_limit_bytes=4 << 20),
    )(coherence, pair)
    return coherence[None], pair[None]


def solution(mesh):
    in_specs = (P(None, "date", None, "range"), P("date"), P("date"), P("date", "range", None))
    out_specs = (P("date", "range", None, None), P("date", "range", None, None, None))
    return jax.shard_map(
        on_device, mesh=mesh, in_specs=in_specs, out_specs=out_specs, check_vma=False
    )
```

```python
import functools

import jax
import jax.numpy as jnp
from jax import lax
from jax.experimental import pallas as pl
from jax.experimental.pallas import tpu as pltpu
from jax.sharding import PartitionSpec as P

MESH = pl.DeviceIdType.MESH
PEERS = 32
RANGE = 16
LOOKS = 20
CHUNKS = ((1, 2, 3), (0, 4))


def sin_pi(r):
    q = r * r
    total = jnp.full_like(q, 0.000466302805767612)
    for c in (-0.00737043094571435, 0.0821458866111282, -0.599264529320792, 2.55016403987735, -5.16771278004997):
        total = total * q + c
    return r * (total * q + 3.14159265358979)


def sinc(x):
    whole = jnp.round(x)
    odd = whole - 2.0 * jnp.floor(whole * 0.5)
    value = sin_pi(x - whole) * (1.0 - 2.0 * odd)
    zero = x == 0.0
    return jnp.where(zero, 1.0, value / jnp.where(zero, 1.0, x * 3.14159265358979))


def lanczos(x):
    return jnp.where(jnp.abs(x) < 4.0, sinc(x) * sinc(x * 0.25), 0.0)


def iota(shape, dim):
    return lax.broadcasted_iota(jnp.int32, shape, dim)


def band_matrices(row_ref, col_ref, col_band, row_band):
    sub, lane = iota((8, 128), 0), iota((8, 128), 1)
    offset = jnp.zeros((8, 128), jnp.int32)
    for date in range(4):
        offset = jnp.where(sub == date, col_ref[date], offset)
        offset = jnp.where(sub == date + 4, row_ref[date], offset)
    place = jnp.where(lane >= 64, lane - 128, lane)
    tap = jnp.where(sub < 4, -place, place)
    weights = lanczos(offset.astype(jnp.float32) * 0.125 - tap.astype(jnp.float32))
    distance = iota((128, 128), 0) - iota((128, 128), 1)
    inside = jnp.abs(distance) <= 5
    first = sub < 4
    reach = [jnp.abs(lane - 4 * m - sub % 4) <= 5 for m in range(32)]
    for date in range(4):
        line = jnp.broadcast_to(weights[date : date + 1], (8, 128))
        base = pltpu.roll(line, 0, 1, stride=1, stride_axis=0)
        ring = jnp.concatenate([base if b == 0 else pltpu.roll(base, 8 * b, 1) for b in range(16)], axis=0)
        col_band[date, :128] = jnp.where(inside, ring, 0.0).astype(jnp.bfloat16)
        col_band[date, 128:] = jnp.where(inside, 0.0, ring).astype(jnp.bfloat16)
        line = jnp.broadcast_to(weights[date + 4 : date + 5], (8, 128))
        base = pltpu.roll(line, 0, 1, stride=1, stride_axis=0)
        base = jnp.where(first, base, pltpu.roll(base, 124, 1))
        real, imag = [], []
        for m in range(32):
            ring = base if m == 0 else pltpu.roll(base, 4 * m, 1)
            real.append(jnp.where(reach[m] & first, ring, 0.0))
            imag.append(jnp.where(reach[m] & ~first, ring, 0.0))
        row_band[date, :, :128] = jnp.concatenate(real, axis=0).astype(jnp.bfloat16)
        row_band[date, :, 128:] = jnp.concatenate(imag, axis=0).astype(jnp.bfloat16)


def resample(windows, slc, low, high, col_band, row_band, send, ready=None):
    low_lane = iota((128, 128), 1) < 64
    count = len(windows)
    for pair in range(2):
        results = []
        for date in (2 * pair, 2 * pair + 1):
            if ready is not None:
                ready[date].wait()
            left = []
            for window in windows:
                for part in range(2):
                    def block(index):
                        return slc[part, date, :, index * 128 : index * 128 + 128]
                    before = low[part, date] if window == 0 else block(window - 1)
                    after = high[part, date] if window == 4 else block(window + 1)
                    rim = jnp.where(low_lane, after, before)
                    left.append(jnp.concatenate([block(window), rim], axis=1))
            left = jnp.concatenate(left, axis=0)
            across = jnp.dot(left, col_band[date], preferred_element_type=jnp.float32).astype(jnp.bfloat16)
            across = jnp.concatenate([across[i * 256 : i * 256 + 256] for i in range(count)], axis=1)
            lines = jnp.dot(row_band[date], across, preferred_element_type=jnp.float32)
            results.append(lines.reshape(PEERS, 8, 128 * count))
        both = jnp.concatenate(results, axis=1)
        send[:, 16 * pair : 16 * pair + 16, :] = both.astype(jnp.bfloat16)


def gather_rows(windows, recv, swap, stack):
    lanes = 128 * len(windows)
    low = iota((64, 128), 1) < 64
    for group in range(4):
        block = recv[8 * group : 8 * group + 8].reshape(256, lanes)
        rows = jnp.dot(swap[...], block, preferred_element_type=jnp.float32)
        for place, window in enumerate(windows):
            for pair in range(2):
                first = rows[128 * pair : 128 * pair + 64, place * 128 : place * 128 + 128]
                second = rows[128 * pair + 64 : 128 * pair + 128, place * 128 : place * 128 + 128]
                second = pltpu.roll(second, 64, 1)
                for half in range(2):
                    mixed = jnp.where(low, second, first) if half else jnp.where(low, first, second)
                    mixed = mixed.astype(jnp.bfloat16)
                    for part in range(2):
                        to = part * 128 + group * 32
                        stack[2 * window + half, to : to + 32, pair * 128 : pair * 128 + 128] = mixed[
                            part * 32 : part * 32 + 32
                        ]


def pixel(index, stack, valid, out, pair):
    gram = None
    lane = iota((1, 256), 1) % 64
    for half in range(index * LOOKS // 64, (index * LOOKS + LOOKS - 1) // 64 + 1):
        start = index * LOOKS - half * 64
        mask = jnp.where((lane >= start) & (lane < start + LOOKS), 1.0, 0.0).astype(jnp.bfloat16)
        rows = stack[half]
        term = lax.dot_general(
            rows * mask, rows, (((1,), (1,)), ((), ())), preferred_element_type=jnp.float32
        )
        gram = term if gram is None else gram + term
    real = gram[:128, :128] + gram[128:, 128:]
    imag = gram[128:, :128] - gram[:128, 128:]
    sub, col = iota((8, 128), 0), iota((8, 128), 1)
    block = (sub - col) >> 3
    step = (sub - col) & 7
    near_re = jnp.zeros((8, 128), jnp.float32)
    near_im = jnp.zeros((8, 128), jnp.float32)
    for b in range(16):
        near_re = jnp.where(block == -b, real[8 * b : 8 * b + 8], near_re)
        near_im = jnp.where(block == -b, imag[8 * b : 8 * b + 8], near_im)

    def diagonal(near, k):
        return jnp.sum(jnp.where(step == k, near, 0.0), axis=0, keepdims=True)

    power = diagonal(near_re, 0) + 8e-5
    mask = valid[pl.ds(index, 1), :].astype(jnp.float32)
    scale = lax.rsqrt(power) * mask
    square = scale * scale
    eye = iota((128, 128), 0) == iota((128, 128), 1)
    down = jnp.sum(jnp.where(eye, jnp.broadcast_to(square, (128, 128)), 0.0), axis=1, keepdims=True)
    value = (real * real + imag * imag) * square * down
    out[index] = jnp.where(value > 0.0, value * lax.rsqrt(value), 0.0).astype(jnp.bfloat16)
    pieces = []
    for k in range(1, 5):
        both = scale * pltpu.roll(scale, 128 - k, 1)
        pieces.append(diagonal(near_re, k) * both)
        pieces.append(-diagonal(near_im, k) * both)
    pair[index] = jnp.concatenate(pieces, axis=0).reshape(4, 2, 128)


def kernel(
    row_in, col_in, slc_in, valid_in, out, pair,
    row_ref, col_ref, slc, valid, in_sem,
    low, high, col_band, row_band, swap, send_a, send_b, recv_a, recv_b, stack,
    halo_sem, send_sem, recv_sem, own_sem,
):
    date = lax.axis_index("date")
    spot = lax.axis_index("range")
    right = lax.rem(spot + 1, RANGE)
    left = lax.rem(spot + RANGE - 1, RANGE)
    barrier = pltpu.get_barrier_semaphore()
    for to in (left, right):
        pl.semaphore_signal(barrier, inc=1, device_id={"range": to}, device_id_type=MESH)

    def greet(step, carry):
        pl.semaphore_signal(
            barrier, inc=1, device_id={"date": lax.rem(date + step, PEERS)}, device_id_type=MESH
        )
        return carry

    lax.fori_loop(1, PEERS, greet, 0)
    loads = [
        pltpu.make_async_copy(source, target, in_sem.at[slot])
        for slot, (source, target) in enumerate(
            (
                (row_in, row_ref),
                (col_in, col_ref),
                *((slc_in.at[:, each], slc.at[:, each]) for each in range(4)),
                (valid_in, valid),
            )
        )
    ]
    for load in loads:
        load.start()
    loads[0].wait()
    loads[1].wait()
    band_matrices(row_ref, col_ref, col_band, row_band)
    sends, recvs = (send_a, send_b), (recv_a, recv_b)
    resample(CHUNKS[0], slc, low, high, col_band, row_band, send_a, loads[2:6])
    pl.semaphore_wait(barrier, PEERS + 1)

    def launch(chunk):
        for z in (0, 1, 4, 2, 5, 3, 6, 7):

            def one(step, carry):
                to = z * 4 + (step ^ (step >> 1))

                @pl.when(to != date)
                def _():
                    pltpu.make_async_remote_copy(
                        src_ref=sends[chunk].at[to],
                        dst_ref=recvs[chunk].at[date],
                        send_sem=send_sem.at[chunk],
                        recv_sem=recv_sem.at[chunk],
                        device_id={"date": to},
                        device_id_type=MESH,
                    ).start()

                return carry

            lax.fori_loop(0, 4, one, 0)
        pltpu.make_async_copy(sends[chunk].at[date], recvs[chunk].at[date], own_sem.at[chunk]).start()

    def landed(chunk):
        pltpu.make_async_copy(
            sends[chunk].at[date], recvs[chunk].at[date], own_sem.at[chunk]
        ).wait()
        some = recvs[chunk].at[pl.ds(0, PEERS - 1)]
        pltpu.make_async_copy(some, some, recv_sem.at[chunk]).wait()

    to_right = pltpu.make_async_remote_copy(
        src_ref=slc.at[:, :, :, pl.ds(512, 128)], dst_ref=low,
        send_sem=halo_sem.at[0], recv_sem=halo_sem.at[1],
        device_id={"range": right}, device_id_type=MESH,
    )
    to_left = pltpu.make_async_remote_copy(
        src_ref=slc.at[:, :, :, pl.ds(0, 128)], dst_ref=high,
        send_sem=halo_sem.at[2], recv_sem=halo_sem.at[3],
        device_id={"range": left}, device_id_type=MESH,
    )
    to_right.start()
    to_left.start()
    launch(0)
    to_right.wait()
    to_left.wait()

    @pl.when(spot == 0)
    def _():
        low[...] = jnp.zeros_like(low)

    @pl.when(spot == RANGE - 1)
    def _():
        high[...] = jnp.zeros_like(high)

    resample(CHUNKS[1], slc, low, high, col_band, row_band, send_b)
    launch(1)

    def pixels(first, last):
        for index in range(first, last):
            pixel(index, stack, valid, out, pair)

    to_row, from_row = iota((256, 256), 0), iota((256, 256), 1)
    source = (to_row % 32) * 8 + (to_row // 32) % 2 * 4 + to_row // 64
    swap[...] = jnp.where(from_row == source, 1.0, 0.0).astype(jnp.bfloat16)
    loads[6].wait()
    landed(0)
    gather_rows(CHUNKS[0], recv_a, swap, stack)
    pixels(7, 25)
    landed(1)
    gather_rows(CHUNKS[1], recv_b, swap, stack)
    pixels(0, 7)
    pixels(25, 32)
    for chunk in range(2):
        some = sends[chunk].at[pl.ds(0, PEERS - 1)]
        pltpu.make_async_copy(some, some, send_sem.at[chunk]).wait()


def hand_over(coherence, pair, coherence_out, pair_out, sem):
    copies = []
    for part in range(4):
        rows = pl.ds(part * 8, 8)
        copies.append(pltpu.make_async_copy(coherence.at[rows], coherence_out.at[rows], sem.at[part]))
    copies.append(pltpu.make_async_copy(pair, pair_out, sem.at[4]))
    for copy in copies:
        copy.start()
    for copy in copies:
        copy.wait()


def on_device(slc, row_offset, col_offset, valid):
    bf16 = jnp.bfloat16
    vmem = pl.BlockSpec(memory_space=pltpu.VMEM)
    hbm = pl.BlockSpec(memory_space=pltpu.HBM)
    blocks = [pltpu.VMEM((PEERS, 32, 128 * len(chunk)), bf16) for chunk in CHUNKS]
    coherence, pair = pl.pallas_call(
        kernel,
        out_shape=(
            pltpu.VMEM((32, 128, 128), bf16),
            pltpu.VMEM((32, 4, 2, 128), jnp.float32),
        ),
        in_specs=[hbm, hbm, hbm, hbm],
        out_specs=(vmem, vmem),
        scratch_shapes=[
            pltpu.SMEM((4,), jnp.int32),
            pltpu.SMEM((4,), jnp.int32),
            pltpu.VMEM((2, 4, 128, 640), bf16),
            pltpu.VMEM((32, 128), jnp.int32),
            pltpu.SemaphoreType.DMA((7,)),
            pltpu.VMEM((2, 4, 128, 128), bf16),
            pltpu.VMEM((2, 4, 128, 128), bf16),
            pltpu.VMEM((4, 256, 128), bf16),
            pltpu.VMEM((4, 256, 256), bf16),
            pltpu.VMEM((256, 256), bf16),
            *blocks,
            *blocks,
            pltpu.VMEM((10, 256, 256), bf16),
            pltpu.SemaphoreType.DMA((4,)),
            pltpu.SemaphoreType.DMA((2,)),
            pltpu.SemaphoreType.DMA((2,)),
            pltpu.SemaphoreType.DMA((2,)),
        ],
        compiler_params=pltpu.CompilerParams(
            collective_id=0, has_side_effects=True, vmem_limit_bytes=60 << 20
        ),
    )(row_offset, col_offset, slc, valid[0])
    hbm = pl.BlockSpec(memory_space=pltpu.HBM)
    coherence, pair = pl.pallas_call(
        hand_over,
        out_shape=(
            jax.ShapeDtypeStruct((32, 128, 128), bf16),
            jax.ShapeDtypeStruct((32, 4, 2, 128), jnp.float32),
        ),
        in_specs=[vmem, vmem],
        out_specs=(hbm, hbm),
        scratch_shapes=[pltpu.SemaphoreType.DMA((5,))],
        compiler_params=pltpu.CompilerParams(vmem_limit_bytes=4 << 20),
    )(coherence, pair)
    return coherence[None], pair[None]


def solution(mesh):
    in_specs = (P(None, "date", None, "range"), P("date"), P("date"), P("date", "range", None))
    out_specs = (P("date", "range", None, None), P("date", "range", None, None, None))
    return jax.shard_map(
        on_device, mesh=mesh, in_specs=in_specs, out_specs=out_specs, check_vma=False
    )
```

```python
import functools

import jax
import jax.numpy as jnp
from jax import lax
from jax.experimental import pallas as pl
from jax.experimental.pallas import tpu as pltpu
from jax.sharding import PartitionSpec as P

MESH = pl.DeviceIdType.MESH
PEERS = 32
RANGE = 16
LOOKS = 20
CHUNKS = ((1, 2, 3), (0, 4))


def sin_pi(r):
    q = r * r
    total = jnp.full_like(q, 0.000466302805767612)
    for c in (-0.00737043094571435, 0.0821458866111282, -0.599264529320792, 2.55016403987735, -5.16771278004997):
        total = total * q + c
    return r * (total * q + 3.14159265358979)


def sinc(x):
    whole = jnp.round(x)
    odd = whole - 2.0 * jnp.floor(whole * 0.5)
    value = sin_pi(x - whole) * (1.0 - 2.0 * odd)
    zero = x == 0.0
    return jnp.where(zero, 1.0, value / jnp.where(zero, 1.0, x * 3.14159265358979))


def lanczos(x):
    return jnp.where(jnp.abs(x) < 4.0, sinc(x) * sinc(x * 0.25), 0.0)


def iota(shape, dim):
    return lax.broadcasted_iota(jnp.int32, shape, dim)


def band_matrices(row_ref, col_ref, col_band, row_band):
    sub, lane = iota((8, 128), 0), iota((8, 128), 1)
    offset = jnp.zeros((8, 128), jnp.int32)
    for date in range(4):
        offset = jnp.where(sub == date, col_ref[date], offset)
        offset = jnp.where(sub == date + 4, row_ref[date], offset)
    place = jnp.where(lane >= 64, lane - 128, lane)
    tap = jnp.where(sub < 4, -place, place)
    weights = lanczos(offset.astype(jnp.float32) * 0.125 - tap.astype(jnp.float32))
    distance = iota((128, 128), 0) - iota((128, 128), 1)
    inside = jnp.abs(distance) <= 5
    first = sub < 4
    reach = [jnp.abs(lane - 4 * m - sub % 4) <= 5 for m in range(32)]
    for date in range(4):
        line = jnp.broadcast_to(weights[date : date + 1], (8, 128))
        base = pltpu.roll(line, 0, 1, stride=1, stride_axis=0)
        ring = jnp.concatenate([base if b == 0 else pltpu.roll(base, 8 * b, 1) for b in range(16)], axis=0)
        col_band[date, :128] = jnp.where(inside, ring, 0.0).astype(jnp.bfloat16)
        col_band[date, 128:] = jnp.where(inside, 0.0, ring).astype(jnp.bfloat16)
        line = jnp.broadcast_to(weights[date + 4 : date + 5], (8, 128))
        base = pltpu.roll(line, 0, 1, stride=1, stride_axis=0)
        base = jnp.where(first, base, pltpu.roll(base, 124, 1))
        real, imag = [], []
        for m in range(32):
            ring = base if m == 0 else pltpu.roll(base, 4 * m, 1)
            real.append(jnp.where(reach[m] & first, ring, 0.0))
            imag.append(jnp.where(reach[m] & ~first, ring, 0.0))
        row_band[date, :, :128] = jnp.concatenate(real, axis=0).astype(jnp.bfloat16)
        row_band[date, :, 128:] = jnp.concatenate(imag, axis=0).astype(jnp.bfloat16)


def resample(windows, slc, low, high, col_band, row_band, send):
    low_lane = iota((128, 128), 1) < 64
    count = len(windows)
    for pair in range(2):
        results = []
        for date in (2 * pair, 2 * pair + 1):
            left = []
            for window in windows:
                for part in range(2):
                    def block(index):
                        return slc[part, date, :, index * 128 : index * 128 + 128]
                    before = low[part, date] if window == 0 else block(window - 1)
                    after = high[part, date] if window == 4 else block(window + 1)
                    rim = jnp.where(low_lane, after, before)
                    left.append(jnp.concatenate([block(window), rim], axis=1))
            left = jnp.concatenate(left, axis=0)
            across = jnp.dot(left, col_band[date], preferred_element_type=jnp.float32).astype(jnp.bfloat16)
            across = jnp.concatenate([across[i * 256 : i * 256 + 256] for i in range(count)], axis=1)
            lines = jnp.dot(row_band[date], across, preferred_element_type=jnp.float32)
            results.append(lines.reshape(PEERS, 8, 128 * count))
        both = jnp.concatenate(results, axis=1)
        send[:, 16 * pair : 16 * pair + 16, :] = both.astype(jnp.bfloat16)


def gather_rows(windows, recv, swap, stack):
    lanes = 128 * len(windows)
    low = iota((64, 128), 1) < 64
    for group in range(4):
        block = recv[8 * group : 8 * group + 8].reshape(256, lanes)
        rows = jnp.dot(swap[...], block, preferred_element_type=jnp.float32)
        for place, window in enumerate(windows):
            for pair in range(2):
                first = rows[128 * pair : 128 * pair + 64, place * 128 : place * 128 + 128]
                second = rows[128 * pair + 64 : 128 * pair + 128, place * 128 : place * 128 + 128]
                second = pltpu.roll(second, 64, 1)
                for half in range(2):
                    mixed = jnp.where(low, second, first) if half else jnp.where(low, first, second)
                    mixed = mixed.astype(jnp.bfloat16)
                    for part in range(2):
                        to = part * 128 + group * 32
                        stack[2 * window + half, to : to + 32, pair * 128 : pair * 128 + 128] = mixed[
                            part * 32 : part * 32 + 32
                        ]


def pixel(index, stack, valid, out, pair):
    gram = None
    lane = iota((1, 256), 1) % 64
    for half in range(index * LOOKS // 64, (index * LOOKS + LOOKS - 1) // 64 + 1):
        start = index * LOOKS - half * 64
        mask = jnp.where((lane >= start) & (lane < start + LOOKS), 1.0, 0.0).astype(jnp.bfloat16)
        rows = stack[half]
        term = lax.dot_general(
            rows * mask, rows, (((1,), (1,)), ((), ())), preferred_element_type=jnp.float32
        )
        gram = term if gram is None else gram + term
    real = gram[:128, :128] + gram[128:, 128:]
    imag = gram[128:, :128] - gram[:128, 128:]
    sub, col = iota((8, 128), 0), iota((8, 128), 1)
    block = (sub - col) >> 3
    step = (sub - col) & 7
    near_re = jnp.zeros((8, 128), jnp.float32)
    near_im = jnp.zeros((8, 128), jnp.float32)
    for b in range(16):
        near_re = jnp.where(block == -b, real[8 * b : 8 * b + 8], near_re)
        near_im = jnp.where(block == -b, imag[8 * b : 8 * b + 8], near_im)

    def diagonal(near, k):
        return jnp.sum(jnp.where(step == k, near, 0.0), axis=0, keepdims=True)

    power = diagonal(near_re, 0) + 8e-5
    mask = valid[pl.ds(index, 1), :].astype(jnp.float32)
    scale = lax.rsqrt(power) * mask
    square = scale * scale
    eye = iota((128, 128), 0) == iota((128, 128), 1)
    down = jnp.sum(jnp.where(eye, jnp.broadcast_to(square, (128, 128)), 0.0), axis=1, keepdims=True)
    value = (real * real + imag * imag) * square * down
    out[index] = jnp.where(value > 0.0, value * lax.rsqrt(value), 0.0).astype(jnp.bfloat16)
    pieces = []
    for k in range(1, 5):
        both = scale * pltpu.roll(scale, 128 - k, 1)
        pieces.append(diagonal(near_re, k) * both)
        pieces.append(-diagonal(near_im, k) * both)
    pair[index] = jnp.concatenate(pieces, axis=0).reshape(4, 2, 128)


def kernel(
    row_in, col_in, slc_in, valid_in, out, pair,
    row_ref, col_ref, slc, valid, in_sem,
    low, high, col_band, row_band, swap, send_a, send_b, recv_a, recv_b, stack,
    halo_sem, send_sem, recv_sem, own_sem,
):
    date = lax.axis_index("date")
    spot = lax.axis_index("range")
    right = lax.rem(spot + 1, RANGE)
    left = lax.rem(spot + RANGE - 1, RANGE)
    barrier = pltpu.get_barrier_semaphore()
    for to in (left, right):
        pl.semaphore_signal(barrier, inc=1, device_id={"range": to}, device_id_type=MESH)

    def greet(step, carry):
        pl.semaphore_signal(
            barrier, inc=1, device_id={"date": lax.rem(date + step, PEERS)}, device_id_type=MESH
        )
        return carry

    lax.fori_loop(1, PEERS, greet, 0)
    loads = [
        pltpu.make_async_copy(source, target, in_sem.at[slot])
        for slot, (source, target) in enumerate(
            ((row_in, row_ref), (col_in, col_ref), (slc_in, slc), (valid_in, valid))
        )
    ]
    for load in loads:
        load.start()
    loads[0].wait()
    loads[1].wait()
    band_matrices(row_ref, col_ref, col_band, row_band)
    loads[2].wait()
    loads[3].wait()
    sends, recvs = (send_a, send_b), (recv_a, recv_b)
    resample(CHUNKS[0], slc, low, high, col_band, row_band, send_a)
    pl.semaphore_wait(barrier, PEERS + 1)

    def launch(chunk):
        for z in (0, 1, 4, 2, 5, 3, 6, 7):

            def one(step, carry):
                to = z * 4 + (step ^ (step >> 1))

                @pl.when(to != date)
                def _():
                    pltpu.make_async_remote_copy(
                        src_ref=sends[chunk].at[to],
                        dst_ref=recvs[chunk].at[date],
                        send_sem=send_sem.at[chunk],
                        recv_sem=recv_sem.at[chunk],
                        device_id={"date": to},
                        device_id_type=MESH,
                    ).start()

                return carry

            lax.fori_loop(0, 4, one, 0)
        pltpu.make_async_copy(sends[chunk].at[date], recvs[chunk].at[date], own_sem.at[chunk]).start()

    def landed(chunk):
        pltpu.make_async_copy(
            sends[chunk].at[date], recvs[chunk].at[date], own_sem.at[chunk]
        ).wait()
        some = recvs[chunk].at[pl.ds(0, PEERS - 1)]
        pltpu.make_async_copy(some, some, recv_sem.at[chunk]).wait()

    to_right = pltpu.make_async_remote_copy(
        src_ref=slc.at[:, :, :, pl.ds(512, 128)], dst_ref=low,
        send_sem=halo_sem.at[0], recv_sem=halo_sem.at[1],
        device_id={"range": right}, device_id_type=MESH,
    )
    to_left = pltpu.make_async_remote_copy(
        src_ref=slc.at[:, :, :, pl.ds(0, 128)], dst_ref=high,
        send_sem=halo_sem.at[2], recv_sem=halo_sem.at[3],
        device_id={"range": left}, device_id_type=MESH,
    )
    to_right.start()
    to_left.start()
    launch(0)
    to_right.wait()
    to_left.wait()

    @pl.when(spot == 0)
    def _():
        low[...] = jnp.zeros_like(low)

    @pl.when(spot == RANGE - 1)
    def _():
        high[...] = jnp.zeros_like(high)

    resample(CHUNKS[1], slc, low, high, col_band, row_band, send_b)
    launch(1)

    def pixels(first, last):
        for index in range(first, last):
            pixel(index, stack, valid, out, pair)

    to_row, from_row = iota((256, 256), 0), iota((256, 256), 1)
    source = (to_row % 32) * 8 + (to_row // 32) % 2 * 4 + to_row // 64
    swap[...] = jnp.where(from_row == source, 1.0, 0.0).astype(jnp.bfloat16)
    landed(0)
    gather_rows(CHUNKS[0], recv_a, swap, stack)
    pixels(7, 25)
    landed(1)
    gather_rows(CHUNKS[1], recv_b, swap, stack)
    pixels(0, 7)
    pixels(25, 32)
    for chunk in range(2):
        some = sends[chunk].at[pl.ds(0, PEERS - 1)]
        pltpu.make_async_copy(some, some, send_sem.at[chunk]).wait()


def hand_over(coherence, pair, coherence_out, pair_out, sem):
    copies = []
    for part in range(8):
        rows = pl.ds(part * 4, 4)
        copies.append(pltpu.make_async_copy(coherence.at[rows], coherence_out.at[rows], sem.at[part]))
    copies.append(pltpu.make_async_copy(pair, pair_out, sem.at[8]))
    for copy in copies:
        copy.start()
    for copy in copies:
        copy.wait()


def on_device(slc, row_offset, col_offset, valid):
    bf16 = jnp.bfloat16
    vmem = pl.BlockSpec(memory_space=pltpu.VMEM)
    hbm = pl.BlockSpec(memory_space=pltpu.HBM)
    blocks = [pltpu.VMEM((PEERS, 32, 128 * len(chunk)), bf16) for chunk in CHUNKS]
    coherence, pair = pl.pallas_call(
        kernel,
        out_shape=(
            pltpu.VMEM((32, 128, 128), bf16),
            pltpu.VMEM((32, 4, 2, 128), jnp.float32),
        ),
        in_specs=[hbm, hbm, hbm, hbm],
        out_specs=(vmem, vmem),
        scratch_shapes=[
            pltpu.SMEM((4,), jnp.int32),
            pltpu.SMEM((4,), jnp.int32),
            pltpu.VMEM((2, 4, 128, 640), bf16),
            pltpu.VMEM((32, 128), jnp.int32),
            pltpu.SemaphoreType.DMA((4,)),
            pltpu.VMEM((2, 4, 128, 128), bf16),
            pltpu.VMEM((2, 4, 128, 128), bf16),
            pltpu.VMEM((4, 256, 128), bf16),
            pltpu.VMEM((4, 256, 256), bf16),
            pltpu.VMEM((256, 256), bf16),
            *blocks,
            *blocks,
            pltpu.VMEM((10, 256, 256), bf16),
            pltpu.SemaphoreType.DMA((4,)),
            pltpu.SemaphoreType.DMA((2,)),
            pltpu.SemaphoreType.DMA((2,)),
            pltpu.SemaphoreType.DMA((2,)),
        ],
        compiler_params=pltpu.CompilerParams(
            collective_id=0, has_side_effects=True, vmem_limit_bytes=60 << 20
        ),
    )(row_offset, col_offset, slc, valid[0])
    hbm = pl.BlockSpec(memory_space=pltpu.HBM)
    coherence, pair = pl.pallas_call(
        hand_over,
        out_shape=(
            jax.ShapeDtypeStruct((32, 128, 128), bf16),
            jax.ShapeDtypeStruct((32, 4, 2, 128), jnp.float32),
        ),
        in_specs=[vmem, vmem],
        out_specs=(hbm, hbm),
        scratch_shapes=[pltpu.SemaphoreType.DMA((9,))],
        compiler_params=pltpu.CompilerParams(vmem_limit_bytes=4 << 20),
    )(coherence, pair)
    return coherence[None], pair[None]


def solution(mesh):
    in_specs = (P(None, "date", None, "range"), P("date"), P("date"), P("date", "range", None))
    out_specs = (P("date", "range", None, None), P("date", "range", None, None, None))
    return jax.shard_map(
        on_device, mesh=mesh, in_specs=in_specs, out_specs=out_specs, check_vma=False
    )
```
